32 devices in a mesh: prow: 4 (over z), pcol: 8 (over y, x, core).
Axes of the slice: x: 2, y: 2, z: 4, core: 2. Of those that a mesh axis runs over, the one named last changes fastest.
Arguments:
- left_vecs: bfloat16 [16384, 4096], P(('prow', 'pcol'))
- right_vecs: bfloat16 [16384, 4096], P(('prow', 'pcol'))
- primal: bfloat16 [4096, 4096], P(('prow', 'pcol'))
- dual_inverse: bfloat16 [4096, 4096], P(('prow', 'pcol'))
- owner_map: int32 [32], replicated, may hold values from 0 to 31, each once
- panel_index: int32 [1], replicated, may hold values from 0 to 62
Outputs:
- panel_factor: float32 [256, 16384], P('pcol', 'prow')
- ahead_update: float32 [256, 16384], P('pcol', 'prow')
The draws below stay inside these ranges and needn't reach their ends.
All inputs are finite; a program needn't handle non-finite values.
Results may differ from the reference program's by a relative error of at most 0.00067.
Values may be sent and summed in bfloat16 or wider, within the bound.
A program may use at most 128 MiB of HBM per device.

```python
import math
import jax
import jax.numpy as jnp
from jax import lax

ORDER = 4096
PANEL = 256
CON_DEV = 512
CONSTRAINTS = 16384
N_PROW = 4
N_PCOL = 8


def symmetric_draw(key, salt):
    keys = jax.random.split(jax.random.fold_in(key, salt), 2)
    diagonal = jax.random.uniform(keys[0], (ORDER,), jnp.float32, 2.0, 4.0)
    noise = jax.random.normal(keys[1], (ORDER, ORDER), jnp.float32)
    symmetric = (noise + noise.T) * (0.35 / math.sqrt(ORDER))
    return (symmetric + jnp.diag(diagonal)).astype(jnp.bfloat16)


def draw_primal(key, part):
    return symmetric_draw(key, 17)


def draw_dual_inverse(key, part):
    return symmetric_draw(key, 29)


def unit_draw(key, shape):
    return jax.random.normal(key, shape, jnp.float32)


def constraint_draw(key, salt):
    shared_key = jax.random.fold_in(key, 101)
    member_keys = jax.random.split(jax.random.fold_in(key, salt), 2)
    scale = 1.0 / math.sqrt(ORDER)
    directions = unit_draw(shared_key, (8, ORDER)) * scale
    weights_mix = unit_draw(member_keys[0], (CONSTRAINTS, 8)) * (1.0 / math.sqrt(8.0))
    mixed = unit_draw(member_keys[1], (CONSTRAINTS, ORDER)) * (0.7 * scale)
    for direction_num in range(8):
        mixed = mixed + 0.7 * weights_mix[:, direction_num:direction_num + 1] * directions[direction_num][None, :]
    limit = 6.0 * scale
    return jnp.clip(mixed, -limit, limit).astype(jnp.bfloat16)


def draw_left_vecs(key, part):
    return constraint_draw(key, 11)


def draw_right_vecs(key, part):
    return constraint_draw(key, 13)


def setup_inputs(seed: int = 0) -> dict:
    key_of = jax.random.split(jax.random.key(seed), 7)
    left_vecs = draw_left_vecs(jax.random.fold_in(key_of[6], 71), 0)
    right_vecs = draw_right_vecs(jax.random.fold_in(key_of[6], 71), 0)
    primal = draw_primal(jax.random.fold_in(key_of[6], 71), 0)
    dual_inverse = draw_dual_inverse(jax.random.fold_in(key_of[6], 71), 0)
    owner_map = jax.random.permutation(key_of[4], N_PROW * N_PCOL).astype(jnp.int32)
    panel_index = jax.random.randint(key_of[5], (1,), 0, CONSTRAINTS // PANEL - 1).astype(jnp.int32)
    return {"left_vecs": left_vecs, "right_vecs": right_vecs, "primal": primal, "dual_inverse": dual_inverse, "owner_map": owner_map, "panel_index": panel_index}


def combine(left_prod, right_prod):
    seg = 2 * PANEL
    return left_prod[:, seg:2 * seg] * right_prod[:, 2 * seg:3 * seg] + right_prod[:, seg:2 * seg] * left_prod[:, 2 * seg:3 * seg] + left_prod[:, 0:seg] * right_prod[:, 3 * seg:4 * seg] + right_prod[:, 0:seg] * left_prod[:, 3 * seg:4 * seg]

def cyclic(matrix):
    blocks = CONSTRAINTS // (PANEL * N_PROW)
    return matrix.reshape(blocks, N_PROW, PANEL, PANEL).transpose(1, 0, 2, 3).reshape(CONSTRAINTS, PANEL).T

def reference(left_vecs, right_vecs, primal, dual_inverse, owner_map, panel_index):
    devices = N_PROW * N_PCOL
    order_idx = jnp.arange(CONSTRAINTS, dtype=jnp.int32)
    sources = (jnp.take(owner_map, order_idx % devices) * CON_DEV + order_idx // devices).astype(jnp.int32)
    start = (panel_index[0] * PANEL).astype(jnp.int32)
    zero_idx = jnp.zeros((), jnp.int32)
    picked = jnp.take(sources, start + jnp.arange(2 * PANEL, dtype=jnp.int32))
    vectors = jnp.concatenate([jnp.take(left_vecs, picked, axis=0), jnp.take(right_vecs, picked, axis=0)], axis=0)
    primal_img = jnp.dot(primal.astype(jnp.float32), vectors.T.astype(jnp.float32), preferred_element_type=jnp.float32)
    dual_img = jnp.dot(dual_inverse.astype(jnp.float32), vectors.T.astype(jnp.float32), preferred_element_type=jnp.float32)
    images = jnp.concatenate([primal_img, dual_img], axis=1).astype(jnp.bfloat16)

    def form(block):
        begin = (block * CON_DEV).astype(jnp.int32)
        rows = lax.dynamic_slice_in_dim(sources, begin, CON_DEV)
        left_prod = jnp.dot(jnp.take(left_vecs, rows, axis=0).astype(jnp.float32), images.astype(jnp.float32), preferred_element_type=jnp.float32)
        right_prod = jnp.dot(jnp.take(right_vecs, rows, axis=0).astype(jnp.float32), images.astype(jnp.float32), preferred_element_type=jnp.float32)
        return combine(left_prod, right_prod)
    schur = lax.map(form, jnp.arange(devices, dtype=jnp.int32)).reshape(CONSTRAINTS, 2 * PANEL)
    base = lax.dynamic_slice(schur, (start, zero_idx), (PANEL, PANEL))
    chol = jnp.linalg.cholesky(base)
    inverse = lax.linalg.triangular_solve(chol, jnp.eye(PANEL, dtype=jnp.float32), left_side=True, lower=True)
    full = jnp.dot(schur[:, :PANEL].astype(jnp.float32), inverse.T.astype(jnp.float32), precision=lax.Precision.HIGHEST, preferred_element_type=jnp.float32)
    full = jnp.where((order_idx >= start)[:, None], full, jnp.float32(0.0))
    ahead_start = (start + PANEL).astype(jnp.int32)
    ahead = lax.dynamic_slice(full, (ahead_start, zero_idx), (PANEL, PANEL))
    update = schur[:, PANEL:] - jnp.dot(full.astype(jnp.float32), ahead.T.astype(jnp.float32), precision=lax.Precision.HIGHEST, preferred_element_type=jnp.float32)
    update = jnp.where((order_idx >= ahead_start)[:, None], update, jnp.float32(0.0))
    return (cyclic(full), cyclic(update))
```

```python
import jax
import jax.numpy as jnp
from jax import lax
from jax.experimental import pallas as pl
from jax.experimental.pallas import tpu as pltpu
from jax.sharding import PartitionSpec as P

PANEL = 256
BLOCK = 64
HIGH = lax.Precision.HIGHEST
F32 = jnp.float32


def combine(left_prod, right_prod):
    seg = left_prod.shape[1] // 4
    return (
        left_prod[:, seg : 2 * seg] * right_prod[:, 2 * seg : 3 * seg]
        + right_prod[:, seg : 2 * seg] * left_prod[:, 2 * seg : 3 * seg]
        + left_prod[:, 0:seg] * right_prod[:, 3 * seg : 4 * seg]
        + right_prod[:, 0:seg] * left_prod[:, 3 * seg : 4 * seg]
    )


def invert_kernel(block_ref, coef_ref, work):
    base = block_ref[:PANEL, :]
    work[:, :PANEL] = 0.5 * (base + base.T)
    rows = lax.broadcasted_iota(jnp.int32, (PANEL, PANEL), 0)
    cols = lax.broadcasted_iota(jnp.int32, (PANEL, PANEL), 1)
    work[:, PANEL:] = jnp.where(rows == cols, 1.0, 0.0).astype(F32)
    row = lax.broadcasted_iota(jnp.int32, (BLOCK, 1), 0)
    brow = lax.broadcasted_iota(jnp.int32, (BLOCK, BLOCK), 0)
    bcol = lax.broadcasted_iota(jnp.int32, (BLOCK, BLOCK), 1)
    eye = jnp.where(brow == bcol, 1.0, 0.0).astype(F32)
    for b in range(PANEL // BLOCK):
        lo = b * BLOCK
        hi = lo + BLOCK
        pair = jnp.concatenate([work[lo:hi, lo:hi], eye], axis=1)
        for k in range(BLOCK):
            pivot = pair[k : k + 1, :]
            scaled = pivot / pair[k : k + 1, k : k + 1]
            factor = jnp.where(row > k, pair[:, k : k + 1], 0.0)
            pair = pair - factor * scaled
        diag = jnp.sum(pair[:, :BLOCK] * eye, axis=1, keepdims=True)
        inv = pair[:, BLOCK:] / jnp.sqrt(diag)
        done = jnp.dot(inv, work[lo:hi, :], precision=HIGH, preferred_element_type=F32)
        work[lo:hi, :] = done
        if hi < PANEL:
            lower = done[:, :PANEL]
            step = lax.dot_general(
                lower, done, (((0,), (0,)), ((), ())), precision=HIGH, preferred_element_type=F32
            )
            work[hi:, :] = work[hi:, :] - step[hi:, :]
    inverse = work[:, PANEL:]
    coef_ref[:PANEL, :] = inverse
    ahead = lax.dot_general(
        block_ref[PANEL:, :],
        inverse,
        (((1,), (1,)), ((), ())),
        precision=HIGH,
        preferred_element_type=F32,
    )
    coef_ref[PANEL:, :] = jnp.dot(ahead, inverse, precision=HIGH, preferred_element_type=F32)


def coefficients(panel_block):
    return pl.pallas_call(
        invert_kernel,
        out_shape=jax.ShapeDtypeStruct((2 * PANEL, PANEL), F32),
        in_specs=[pl.BlockSpec(memory_space=pltpu.VMEM)],
        out_specs=pl.BlockSpec(memory_space=pltpu.VMEM),
        scratch_shapes=[pltpu.VMEM((PANEL, 2 * PANEL), F32)],
        compiler_params=pltpu.CompilerParams(vmem_limit_bytes=16 * 1024 * 1024),
    )(panel_block)


def body(left_vecs, right_vecs, primal, dual_inverse, owner_map, panel_index):
    devices = lax.axis_size(("prow", "pcol"))
    grid_rows = lax.axis_size("prow")
    grid_cols = lax.axis_size("pcol")
    height = PANEL // devices
    slots = left_vecs.shape[0]
    order = left_vecs.shape[1]
    feats = primal.shape[0]
    start = panel_index[0] * PANEL
    first_slot = start // devices
    wide = lax.broadcasted_iota(jnp.int32, (devices, height, height, devices), 0)
    perm = (wide == owner_map[None, None, None, :]) & (
        lax.broadcasted_iota(jnp.int32, wide.shape, 1)
        == lax.broadcasted_iota(jnp.int32, wide.shape, 2)
    )
    perm = perm.astype(jnp.bfloat16).reshape(PANEL, PANEL)
    perm32 = perm.astype(F32)

    panel_left = lax.dynamic_slice_in_dim(left_vecs, first_slot, 2 * height, 0)
    panel_right = lax.dynamic_slice_in_dim(right_vecs, first_slot, 2 * height, 0)
    own_vecs = jnp.concatenate([panel_left, panel_right], axis=0)
    panel_vecs = lax.all_gather(own_vecs, ("prow", "pcol"), axis=0, tiled=True)
    matrices = jnp.concatenate([primal, dual_inverse], axis=0)
    raw = lax.dot_general(
        panel_vecs, matrices, (((1,), (1,)), ((), ())), preferred_element_type=F32
    )
    raw = raw.reshape(devices, 4, height, 2 * feats).transpose(1, 0, 2, 3)
    raw = raw.reshape(4, PANEL, 2, feats).astype(jnp.bfloat16)
    images = jnp.einsum("vkgf,kj->fgvj", raw, perm, preferred_element_type=F32)
    images = images.astype(jnp.bfloat16).reshape(feats, 8 * PANEL)
    piece = lax.all_gather(images, ("prow", "pcol"), axis=0, tiled=True)
    left_prod = jnp.dot(left_vecs, piece, preferred_element_type=F32)
    right_prod = jnp.dot(right_vecs, piece, preferred_element_type=F32)
    schur = combine(left_prod, right_prod)

    own_panel = lax.dynamic_slice_in_dim(schur[:, :PANEL], first_slot, 2 * height, 0)
    panel_rows = lax.all_gather(own_panel, ("prow", "pcol"), axis=0, tiled=True)
    panel_rows = panel_rows.reshape(devices, 2, height, PANEL).transpose(1, 0, 2, 3)
    panel_block = jnp.einsum(
        "kj,pkc->pjc",
        perm32,
        panel_rows.reshape(2, PANEL, PANEL),
        precision=HIGH,
        preferred_element_type=F32,
    ).reshape(2 * PANEL, PANEL)
    coef = coefficients(panel_block)

    groups = slots // (grid_rows * height)
    narrow = PANEL // grid_cols
    placed = schur.reshape(groups, grid_rows, height, 2 * PANEL).transpose(1, 2, 0, 3)
    placed = placed.reshape(slots, 2 * PANEL)
    ident = lax.broadcasted_iota(jnp.int32, (grid_rows, height, groups), 0) * height
    ident = ident + lax.broadcasted_iota(jnp.int32, ident.shape, 1)
    ident = ident + lax.broadcasted_iota(jnp.int32, ident.shape, 2) * (grid_rows * height)
    ident = ident.reshape(slots, 1)
    mixed = lax.dot_general(
        placed[:, :PANEL], coef, (((1,), (1,)), ((), ())), precision=HIGH, preferred_element_type=F32
    )
    full = jnp.where(ident >= first_slot, mixed[:, :PANEL], 0.0)
    update = jnp.where(
        ident >= first_slot + height, placed[:, PANEL:] - mixed[:, PANEL:], 0.0
    )
    both = jnp.stack(
        [
            full.reshape(grid_rows, height, groups, grid_cols, narrow),
            update.reshape(grid_rows, height, groups, grid_cols, narrow),
        ],
        axis=4,
    )
    outgoing = both.transpose(0, 3, 1, 2, 4, 5).reshape(devices, height, groups * 2 * narrow)
    arrived = lax.all_to_all(outgoing, ("prow", "pcol"), split_axis=0, concat_axis=0, tiled=True)
    final = lax.dot_general(
        arrived.reshape(PANEL, groups * 2 * narrow),
        perm32,
        (((0,), (0,)), ((), ())),
        precision=HIGH,
        preferred_element_type=F32,
    )
    final = final.reshape(groups, 2, narrow, PANEL).transpose(1, 2, 0, 3)
    final = final.reshape(2, narrow, groups * PANEL)
    return (final[0], final[1])


def solution(mesh):
    return jax.shard_map(
        body,
        mesh=mesh,
        in_specs=(
            P(("prow", "pcol"), None),
            P(("prow", "pcol"), None),
            P(("prow", "pcol"), None),
            P(("prow", "pcol"), None),
            P(),
            P(),
        ),
        out_specs=(P("pcol", "prow"), P("pcol", "prow")),
        check_vma=False,
    )
```

```python
import functools

import jax
import jax.numpy as jnp
from jax import lax
from jax.experimental import pallas as pl
from jax.experimental.pallas import tpu as pltpu
from jax.sharding import PartitionSpec as P

PANEL = 256
BLOCK = 64
HIGH = lax.Precision.HIGHEST
F32 = jnp.float32


def combine(left_prod, right_prod):
    seg = left_prod.shape[1] // 4
    return (
        left_prod[:, seg : 2 * seg] * right_prod[:, 2 * seg : 3 * seg]
        + right_prod[:, seg : 2 * seg] * left_prod[:, 2 * seg : 3 * seg]
        + left_prod[:, 0:seg] * right_prod[:, 3 * seg : 4 * seg]
        + right_prod[:, 0:seg] * left_prod[:, 3 * seg : 4 * seg]
    )


def invert_kernel(block_ref, coef_ref, work):
    base = block_ref[:PANEL, :]
    work[:, :PANEL] = 0.5 * (base + base.T)
    rows = lax.broadcasted_iota(jnp.int32, (PANEL, PANEL), 0)
    cols = lax.broadcasted_iota(jnp.int32, (PANEL, PANEL), 1)
    work[:, PANEL:] = jnp.where(rows == cols, 1.0, 0.0).astype(F32)
    row = lax.broadcasted_iota(jnp.int32, (BLOCK, 1), 0)
    brow = lax.broadcasted_iota(jnp.int32, (BLOCK, BLOCK), 0)
    bcol = lax.broadcasted_iota(jnp.int32, (BLOCK, BLOCK), 1)
    eye = jnp.where(brow == bcol, 1.0, 0.0).astype(F32)
    for b in range(PANEL // BLOCK):
        lo = b * BLOCK
        hi = lo + BLOCK
        pair = jnp.concatenate([work[lo:hi, lo:hi], eye], axis=1)
        for k in range(BLOCK):
            pivot = pair[k : k + 1, :]
            scaled = pivot / pair[k : k + 1, k : k + 1]
            factor = jnp.where(row > k, pair[:, k : k + 1], 0.0)
            pair = pair - factor * scaled
        diag = jnp.sum(pair[:, :BLOCK] * eye, axis=1, keepdims=True)
        inv = pair[:, BLOCK:] / jnp.sqrt(diag)
        done = jnp.dot(inv, work[lo:hi, :], precision=HIGH, preferred_element_type=F32)
        work[lo:hi, :] = done
        if hi < PANEL:
            lower = done[:, :PANEL]
            step = lax.dot_general(
                lower, done, (((0,), (0,)), ((), ())), precision=HIGH, preferred_element_type=F32
            )
            work[hi:, :] = work[hi:, :] - step[hi:, :]
    inverse = work[:, PANEL:]
    coef_ref[:PANEL, :] = inverse
    ahead = lax.dot_general(
        block_ref[PANEL:, :],
        inverse,
        (((1,), (1,)), ((), ())),
        precision=HIGH,
        preferred_element_type=F32,
    )
    coef_ref[PANEL:, :] = jnp.dot(ahead, inverse, precision=HIGH, preferred_element_type=F32)


def coefficients(panel_block):
    return pl.pallas_call(
        invert_kernel,
        out_shape=jax.ShapeDtypeStruct((2 * PANEL, PANEL), F32),
        in_specs=[pl.BlockSpec(memory_space=pltpu.VMEM)],
        out_specs=pl.BlockSpec(memory_space=pltpu.VMEM),
        scratch_shapes=[pltpu.VMEM((PANEL, 2 * PANEL), F32)],
        compiler_params=pltpu.CompilerParams(vmem_limit_bytes=16 * 1024 * 1024),
    )(panel_block)


def gather_kernel(grid_rows, grid_cols, x_ref, out_ref, local_sem, send_sem, recv_sem):
    prow = lax.axis_index("prow")
    pcol = lax.axis_index("pcol")
    chip = pcol // 2
    core = pcol % 2
    across = grid_cols // 4
    side = chip // across
    place = chip % across

    def column(side_at, place_at, core_at):
        return (side_at * across + place_at) * 2 + core_at

    near = sorted(range(1, grid_rows), key=lambda s: (min(s, grid_rows - s), s))
    along = [(lax.rem(prow + s, grid_rows), pcol) for s in near]
    facing = (prow, column(1 - side, place, core))
    beside = [
        (prow, column(side, lax.rem(place + t, across), core)) for t in range(1, across)
    ]
    sibling = (prow, column(side, place, 1 - core))
    barrier = pltpu.get_barrier_semaphore()
    peers = along + [facing] + beside + [sibling]
    for peer in peers:
        pl.semaphore_signal(barrier, inc=1, device_id=peer, device_id_type=pl.DeviceIdType.MESH)
    pl.semaphore_wait(barrier, len(peers))

    sends = []

    def send(src, slot, peer):
        copy = pltpu.make_async_remote_copy(
            src_ref=src,
            dst_ref=out_ref.at[slot],
            send_sem=send_sem.at[len(sends)],
            recv_sem=recv_sem.at[slot],
            device_id=peer,
            device_id_type=pl.DeviceIdType.MESH,
        )
        copy.start()
        sends.append(copy)

    def arrive(slot):
        pltpu.make_async_remote_copy(
            src_ref=out_ref.at[slot],
            dst_ref=out_ref.at[slot],
            send_sem=send_sem.at[0],
            recv_sem=recv_sem.at[slot],
            device_id=sibling,
            device_id_type=pl.DeviceIdType.MESH,
        ).wait_recv()

    def slot_of(row, col, half):
        return (row * grid_cols + col) * 2 + half

    def pass_on(slot, to):
        arrive(slot)
        for peer in to:
            send(out_ref.at[slot], slot, peer)

    mine = slot_of(prow, pcol, 0)
    local = pltpu.make_async_copy(x_ref, out_ref.at[pl.ds(mine, 2)], local_sem)
    local.start()
    for half in range(2):
        for peer in [facing] + beside + along + [sibling]:
            send(x_ref.at[half], mine + half, peer)

    def from_plane(row):
        for half in range(2):
            slot = slot_of(row, facing[1], half)
            pass_on(slot, (beside if half == 0 else []) + [sibling])
            for peer in beside:
                slot = slot_of(row, peer[1], half)
                pass_on(slot, ([facing] if half == 1 else []) + [sibling])

    def from_corner(row):
        for t in range(1, across):
            col = column(1 - side, lax.rem(place + t, across), core)
            for half in range(2):
                pass_on(slot_of(row, col, half), [sibling])

    rows = [prow] + [peer[0] for peer in along]
    for step in range(grid_rows + 2):
        if 0 < step < grid_rows:
            for half in range(2):
                pass_on(slot_of(rows[step], pcol, half), [facing] + beside + [sibling])
        if 1 <= step <= grid_rows:
            from_plane(rows[step - 1])
        if 2 <= step:
            from_corner(rows[step - 2])
    for row in rows:
        for side_at in (side, 1 - side):
            for t in range(across):
                col = column(side_at, lax.rem(place + t, across), 1 - core)
                for half in range(2):
                    arrive(slot_of(row, col, half))
    local.wait()
    for copy in sends:
        copy.wait_send()


def gather(x, collective_id, tile):
    grid_rows = lax.axis_size("prow")
    grid_cols = lax.axis_size("pcol")
    devices = grid_rows * grid_cols
    rows, columns = x.shape
    if grid_cols % 4 or rows % (2 * tile):
        return lax.all_gather(x, ("prow", "pcol"), axis=0, tiled=True)
    across = grid_cols // 4
    count = 2 * (grid_rows - 1 + grid_rows * across + grid_rows * grid_cols // 2)
    count += 2 * grid_rows * (across - 1)
    out = pl.pallas_call(
        functools.partial(gather_kernel, grid_rows, grid_cols),
        out_shape=jax.ShapeDtypeStruct((2 * devices, rows // 2, columns), x.dtype),
        in_specs=[pl.BlockSpec(memory_space=pl.ANY)],
        out_specs=pl.BlockSpec(memory_space=pl.ANY),
        scratch_shapes=[
            pltpu.SemaphoreType.DMA,
            pltpu.SemaphoreType.DMA((count,)),
            pltpu.SemaphoreType.DMA((2 * devices,)),
        ],
        compiler_params=pltpu.CompilerParams(
            collective_id=collective_id, has_side_effects=True
        ),
    )(x.reshape(2, rows // 2, columns))
    return out.reshape(devices * rows, columns)


def body(left_vecs, right_vecs, primal, dual_inverse, owner_map, panel_index):
    devices = lax.axis_size(("prow", "pcol"))
    grid_rows = lax.axis_size("prow")
    grid_cols = lax.axis_size("pcol")
    height = PANEL // devices
    slots = left_vecs.shape[0]
    order = left_vecs.shape[1]
    feats = primal.shape[0]
    start = panel_index[0] * PANEL
    first_slot = start // devices
    wide = lax.broadcasted_iota(jnp.int32, (devices, height, height, devices), 0)
    perm = (wide == owner_map[None, None, None, :]) & (
        lax.broadcasted_iota(jnp.int32, wide.shape, 1)
        == lax.broadcasted_iota(jnp.int32, wide.shape, 2)
    )
    perm = perm.astype(jnp.bfloat16).reshape(PANEL, PANEL)
    perm32 = perm.astype(F32)

    panel_left = lax.dynamic_slice_in_dim(left_vecs, first_slot, 2 * height, 0)
    panel_right = lax.dynamic_slice_in_dim(right_vecs, first_slot, 2 * height, 0)
    own_vecs = jnp.concatenate([panel_left, panel_right], axis=0)
    panel_vecs = gather(own_vecs, 0, 16)
    matrices = jnp.concatenate([primal, dual_inverse], axis=0)
    raw = lax.dot_general(
        panel_vecs, matrices, (((1,), (1,)), ((), ())), preferred_element_type=F32
    )
    raw = raw.reshape(devices, 4, height, 2 * feats).transpose(1, 0, 2, 3)
    raw = raw.reshape(4, PANEL, 2, feats).astype(jnp.bfloat16)
    images = jnp.einsum("vkgf,kj->fgvj", raw, perm, preferred_element_type=F32)
    images = images.astype(jnp.bfloat16).reshape(feats, 8 * PANEL)
    piece = gather(images, 1, 16)
    left_prod = jnp.dot(left_vecs, piece, preferred_element_type=F32)
    right_prod = jnp.dot(right_vecs, piece, preferred_element_type=F32)
    schur = combine(left_prod, right_prod)

    own_panel = lax.dynamic_slice_in_dim(schur[:, :PANEL], first_slot, 2 * height, 0)
    panel_rows = gather(own_panel, 2, 8)
    panel_rows = panel_rows.reshape(devices, 2, height, PANEL).transpose(1, 0, 2, 3)
    panel_block = jnp.einsum(
        "kj,pkc->pjc",
        perm32,
        panel_rows.reshape(2, PANEL, PANEL),
        precision=HIGH,
        preferred_element_type=F32,
    ).reshape(2 * PANEL, PANEL)
    coef = coefficients(panel_block)

    groups = slots // (grid_rows * height)
    narrow = PANEL // grid_cols
    placed = schur.reshape(groups, grid_rows, height, 2 * PANEL).transpose(1, 2, 0, 3)
    placed = placed.reshape(slots, 2 * PANEL)
    ident = lax.broadcasted_iota(jnp.int32, (grid_rows, height, groups), 0) * height
    ident = ident + lax.broadcasted_iota(jnp.int32, ident.shape, 1)
    ident = ident + lax.broadcasted_iota(jnp.int32, ident.shape, 2) * (grid_rows * height)
    ident = ident.reshape(slots, 1)
    mixed = lax.dot_general(
        placed[:, :PANEL], coef, (((1,), (1,)), ((), ())), precision=HIGH, preferred_element_type=F32
    )
    full = jnp.where(ident >= first_slot, mixed[:, :PANEL], 0.0)
    update = jnp.where(
        ident >= first_slot + height, placed[:, PANEL:] - mixed[:, PANEL:], 0.0
    )
    both = jnp.stack(
        [
            full.reshape(grid_rows, height, groups, grid_cols, narrow),
            update.reshape(grid_rows, height, groups, grid_cols, narrow),
        ],
        axis=4,
    )
    outgoing = both.transpose(0, 3, 1, 2, 4, 5).reshape(devices, height, groups * 2 * narrow)
    arrived = lax.all_to_all(outgoing, ("prow", "pcol"), split_axis=0, concat_axis=0, tiled=True)
    final = lax.dot_general(
        arrived.reshape(PANEL, groups * 2 * narrow),
        perm32,
        (((0,), (0,)), ((), ())),
        precision=HIGH,
        preferred_element_type=F32,
    )
    final = final.reshape(groups, 2, narrow, PANEL).transpose(1, 2, 0, 3)
    final = final.reshape(2, narrow, groups * PANEL)
    return (final[0], final[1])


def solution(mesh):
    return jax.shard_map(
        body,
        mesh=mesh,
        in_specs=(
            P(("prow", "pcol"), None),
            P(("prow", "pcol"), None),
            P(("prow", "pcol"), None),
            P(("prow", "pcol"), None),
            P(),
            P(),
        ),
        out_specs=(P("pcol", "prow"), P("pcol", "prow")),
        check_vma=False,
    )
```

```python
import functools

import jax
import jax.numpy as jnp
from jax import lax
from jax.experimental import pallas as pl
from jax.experimental.pallas import tpu as pltpu
from jax.sharding import PartitionSpec as P

PANEL = 256
BLOCK = 64
HIGH = lax.Precision.HIGHEST
F32 = jnp.float32


def combine(left_prod, right_prod):
    seg = left_prod.shape[1] // 4
    return (
        left_prod[:, seg : 2 * seg] * right_prod[:, 2 * seg : 3 * seg]
        + right_prod[:, seg : 2 * seg] * left_prod[:, 2 * seg : 3 * seg]
        + left_prod[:, 0:seg] * right_prod[:, 3 * seg : 4 * seg]
        + right_prod[:, 0:seg] * left_prod[:, 3 * seg : 4 * seg]
    )


def finish_kernel(grid_rows, grid_cols, block_ref, schur_ref, first_ref, out_ref, work, coef_ref, mixed):
    base = block_ref[:PANEL, :]
    work[:, :PANEL] = 0.5 * (base + base.T)
    rows = lax.broadcasted_iota(jnp.int32, (PANEL, PANEL), 0)
    cols = lax.broadcasted_iota(jnp.int32, (PANEL, PANEL), 1)
    work[:, PANEL:] = jnp.where(rows == cols, 1.0, 0.0).astype(F32)
    row = lax.broadcasted_iota(jnp.int32, (BLOCK, 1), 0)
    brow = lax.broadcasted_iota(jnp.int32, (BLOCK, BLOCK), 0)
    bcol = lax.broadcasted_iota(jnp.int32, (BLOCK, BLOCK), 1)
    eye = jnp.where(brow == bcol, 1.0, 0.0).astype(F32)
    for b in range(PANEL // BLOCK):
        lo = b * BLOCK
        hi = lo + BLOCK
        pair = jnp.concatenate([work[lo:hi, lo:hi], eye], axis=1)
        for k in range(BLOCK):
            pivot = pair[k : k + 1, :]
            scaled = pivot / pair[k : k + 1, k : k + 1]
            factor = jnp.where(row > k, pair[:, k : k + 1], 0.0)
            pair = pair - factor * scaled
        diag = jnp.sum(pair[:, :BLOCK] * eye, axis=1, keepdims=True)
        inv = pair[:, BLOCK:] / jnp.sqrt(diag)
        done = jnp.dot(inv, work[lo:hi, :], precision=HIGH, preferred_element_type=F32)
        work[lo:hi, :] = done
        if hi < PANEL:
            lower = done[:, :PANEL]
            step = lax.dot_general(
                lower, done, (((0,), (0,)), ((), ())), precision=HIGH, preferred_element_type=F32
            )
            work[hi:, :] = work[hi:, :] - step[hi:, :]
    inverse = work[:, PANEL:]
    coef_ref[:PANEL, :] = inverse
    ahead = lax.dot_general(
        block_ref[PANEL:, :],
        inverse,
        (((1,), (1,)), ((), ())),
        precision=HIGH,
        preferred_element_type=F32,
    )
    coef_ref[PANEL:, :] = jnp.dot(ahead, inverse, precision=HIGH, preferred_element_type=F32)
    slots = schur_ref.shape[0]
    height = PANEL // (grid_rows * grid_cols)
    groups = slots // (grid_rows * height)
    narrow = PANEL // grid_cols
    first = first_ref[...]
    ident = lax.broadcasted_iota(jnp.int32, (slots, PANEL), 0)
    both = lax.dot_general(
        schur_ref[:, :PANEL],
        coef_ref[...],
        (((1,), (1,)), ((), ())),
        precision=HIGH,
        preferred_element_type=F32,
    )
    mixed[:, :PANEL] = jnp.where(ident >= first, both[:, :PANEL], 0.0)
    mixed[:, PANEL:] = jnp.where(
        ident >= first + height, schur_ref[:, PANEL:] - both[:, PANEL:], 0.0
    )
    if height % 8:
        out_ref[...] = mixed[...]
        return
    run = 128 // narrow
    for prow in range(grid_rows):
        for half in range(2):
            for group in range(0, groups, run):
                tops = [((group + i) * grid_rows + prow) * height for i in range(run)]
                for pcol in range(grid_cols):
                    lo = half * PANEL + pcol * narrow
                    to = (half * groups + group) * narrow
                    out_ref[prow * grid_cols + pcol, :, to : to + 128] = jnp.concatenate(
                        [mixed[top : top + height, lo : lo + narrow] for top in tops], axis=1
                    )


def finish(panel_block, schur, first_slot, grid_rows, grid_cols):
    devices = grid_rows * grid_cols
    slots = schur.shape[0]
    height = PANEL // devices
    groups = slots // (grid_rows * height)
    narrow = PANEL // grid_cols
    tiled = height % 8 == 0
    shape = (devices, height, 2 * groups * narrow) if tiled else (slots, 2 * PANEL)
    out = pl.pallas_call(
        functools.partial(finish_kernel, grid_rows, grid_cols),
        out_shape=jax.ShapeDtypeStruct(shape, F32),
        in_specs=[pl.BlockSpec(memory_space=pltpu.VMEM)] * 3,
        out_specs=pl.BlockSpec(memory_space=pltpu.VMEM),
        scratch_shapes=[
            pltpu.VMEM((PANEL, 2 * PANEL), F32),
            pltpu.VMEM((2 * PANEL, PANEL), F32),
            pltpu.VMEM((slots, 2 * PANEL), F32),
        ],
        compiler_params=pltpu.CompilerParams(vmem_limit_bytes=24 * 1024 * 1024),
    )(panel_block, schur, jnp.full((1, PANEL), first_slot, jnp.int32))
    if tiled:
        return out
    out = out.reshape(groups, grid_rows, height, 2, grid_cols, narrow)
    return out.transpose(1, 4, 2, 3, 0, 5).reshape(devices, height, 2 * groups * narrow)


def gather_kernel(grid_rows, grid_cols, x_ref, out_ref, local_sem, send_sem, recv_sem):
    prow = lax.axis_index("prow")
    pcol = lax.axis_index("pcol")
    chip = pcol // 2
    core = pcol % 2
    across = grid_cols // 4
    side = chip // across
    place = chip % across

    def column(side_at, place_at, core_at):
        return (side_at * across + place_at) * 2 + core_at

    near = sorted(range(1, grid_rows), key=lambda s: (min(s, grid_rows - s), s))
    along = [(lax.rem(prow + s, grid_rows), pcol) for s in near]
    facing = (prow, column(1 - side, place, core))
    beside = [
        (prow, column(side, lax.rem(place + t, across), core)) for t in range(1, across)
    ]
    sibling = (prow, column(side, place, 1 - core))
    barrier = pltpu.get_barrier_semaphore()
    peers = along + [facing] + beside + [sibling]
    for peer in peers:
        pl.semaphore_signal(barrier, inc=1, device_id=peer, device_id_type=pl.DeviceIdType.MESH)
    pl.semaphore_wait(barrier, len(peers))

    sends = []

    def send(src, slot, peer):
        copy = pltpu.make_async_remote_copy(
            src_ref=src,
            dst_ref=out_ref.at[slot],
            send_sem=send_sem.at[len(sends)],
            recv_sem=recv_sem.at[slot],
            device_id=peer,
            device_id_type=pl.DeviceIdType.MESH,
        )
        copy.start()
        sends.append(copy)

    def arrive(slot):
        pltpu.make_async_remote_copy(
            src_ref=out_ref.at[slot],
            dst_ref=out_ref.at[slot],
            send_sem=send_sem.at[0],
            recv_sem=recv_sem.at[slot],
            device_id=sibling,
            device_id_type=pl.DeviceIdType.MESH,
        ).wait_recv()

    def slot_of(row, col, half):
        return (row * grid_cols + col) * 2 + half

    def pass_on(slot, to):
        arrive(slot)
        for peer in to:
            send(out_ref.at[slot], slot, peer)

    mine = slot_of(prow, pcol, 0)
    local = pltpu.make_async_copy(x_ref, out_ref.at[pl.ds(mine, 2)], local_sem)
    local.start()
    for half in range(2):
        for peer in [facing] + beside + along + [sibling]:
            send(x_ref.at[half], mine + half, peer)

    def from_plane(row):
        for half in range(2):
            slot = slot_of(row, facing[1], half)
            pass_on(slot, (beside if half == 0 else []) + [sibling])
            for peer in beside:
                slot = slot_of(row, peer[1], half)
                pass_on(slot, ([facing] if half == 1 else []) + [sibling])

    def from_corner(row):
        for t in range(1, across):
            col = column(1 - side, lax.rem(place + t, across), core)
            for half in range(2):
                pass_on(slot_of(row, col, half), [sibling])

    rows = [prow] + [peer[0] for peer in along]
    for step in range(grid_rows + 2):
        if 0 < step < grid_rows:
            for half in range(2):
                pass_on(slot_of(rows[step], pcol, half), [facing] + beside + [sibling])
        if 1 <= step <= grid_rows:
            from_plane(rows[step - 1])
        if 2 <= step:
            from_corner(rows[step - 2])
    for row in rows:
        for side_at in (side, 1 - side):
            for t in range(across):
                col = column(side_at, lax.rem(place + t, across), 1 - core)
                for half in range(2):
                    arrive(slot_of(row, col, half))
    local.wait()
    for copy in sends:
        copy.wait_send()


def gather(x, collective_id, tile):
    grid_rows = lax.axis_size("prow")
    grid_cols = lax.axis_size("pcol")
    devices = grid_rows * grid_cols
    rows, columns = x.shape
    if grid_cols % 4 or rows % (2 * tile):
        return lax.all_gather(x, ("prow", "pcol"), axis=0, tiled=True)
    across = grid_cols // 4
    count = 2 * (grid_rows - 1 + grid_rows * across + grid_rows * grid_cols // 2)
    count += 2 * grid_rows * (across - 1)
    out = pl.pallas_call(
        functools.partial(gather_kernel, grid_rows, grid_cols),
        out_shape=jax.ShapeDtypeStruct((2 * devices, rows // 2, columns), x.dtype),
        in_specs=[pl.BlockSpec(memory_space=pl.ANY)],
        out_specs=pl.BlockSpec(memory_space=pl.ANY),
        scratch_shapes=[
            pltpu.SemaphoreType.DMA,
            pltpu.SemaphoreType.DMA((count,)),
            pltpu.SemaphoreType.DMA((2 * devices,)),
        ],
        compiler_params=pltpu.CompilerParams(
            collective_id=collective_id, has_side_effects=True
        ),
    )(x.reshape(2, rows // 2, columns))
    return out.reshape(devices * rows, columns)


def body(left_vecs, right_vecs, primal, dual_inverse, owner_map, panel_index):
    devices = lax.axis_size(("prow", "pcol"))
    grid_rows = lax.axis_size("prow")
    grid_cols = lax.axis_size("pcol")
    height = PANEL // devices
    slots = left_vecs.shape[0]
    order = left_vecs.shape[1]
    feats = primal.shape[0]
    start = panel_index[0] * PANEL
    first_slot = start // devices
    wide = lax.broadcasted_iota(jnp.int32, (devices, height, height, devices), 0)
    perm = (wide == owner_map[None, None, None, :]) & (
        lax.broadcasted_iota(jnp.int32, wide.shape, 1)
        == lax.broadcasted_iota(jnp.int32, wide.shape, 2)
    )
    perm = perm.astype(jnp.bfloat16).reshape(PANEL, PANEL)
    perm32 = perm.astype(F32)

    panel_left = lax.dynamic_slice_in_dim(left_vecs, first_slot, 2 * height, 0)
    panel_right = lax.dynamic_slice_in_dim(right_vecs, first_slot, 2 * height, 0)
    own_vecs = jnp.concatenate([panel_left, panel_right], axis=0)
    panel_vecs = gather(own_vecs, 0, 16)
    matrices = jnp.concatenate([primal, dual_inverse], axis=0)
    raw = lax.dot_general(
        panel_vecs, matrices, (((1,), (1,)), ((), ())), preferred_element_type=F32
    )
    raw = raw.reshape(devices, 4, height, 2 * feats).transpose(1, 0, 2, 3)
    raw = raw.reshape(4, PANEL, 2, feats).astype(jnp.bfloat16)
    images = jnp.einsum("vkgf,kj->fgvj", raw, perm, preferred_element_type=F32)
    images = images.astype(jnp.bfloat16).reshape(feats, 8 * PANEL)
    piece = gather(images, 1, 16)
    early = jnp.dot(own_vecs, piece, preferred_element_type=F32)
    own_panel = combine(early[: 2 * height], early[2 * height :])
    panel_rows = lax.all_gather(own_panel, ("prow", "pcol"), axis=0, tiled=True)
    left_prod = jnp.dot(left_vecs, piece, preferred_element_type=F32)
    right_prod = jnp.dot(right_vecs, piece, preferred_element_type=F32)
    schur = combine(left_prod, right_prod)

    panel_rows = panel_rows[:, :PANEL]
    panel_rows = panel_rows.reshape(devices, 2, height, PANEL).transpose(1, 0, 2, 3)
    panel_block = jnp.einsum(
        "kj,pkc->pjc",
        perm32,
        panel_rows.reshape(2, PANEL, PANEL),
        precision=HIGH,
        preferred_element_type=F32,
    ).reshape(2 * PANEL, PANEL)
    groups = slots // (grid_rows * height)
    narrow = PANEL // grid_cols
    outgoing = finish(panel_block, schur, first_slot, grid_rows, grid_cols)
    arrived = lax.all_to_all(outgoing, ("prow", "pcol"), split_axis=0, concat_axis=0, tiled=True)
    final = lax.dot_general(
        arrived.reshape(PANEL, groups * 2 * narrow),
        perm32,
        (((0,), (0,)), ((), ())),
        precision=HIGH,
        preferred_element_type=F32,
    )
    final = final.reshape(2, groups, narrow, PANEL).transpose(0, 2, 1, 3)
    final = final.reshape(2, narrow, groups * PANEL)
    return (final[0], final[1])


def solution(mesh):
    return jax.shard_map(
        body,
        mesh=mesh,
        in_specs=(
            P(("prow", "pcol"), None),
            P(("prow", "pcol"), None),
            P(("prow", "pcol"), None),
            P(("prow", "pcol"), None),
            P(),
            P(),
        ),
        out_specs=(P("pcol", "prow"), P("pcol", "prow")),
        check_vma=False,
    )
```

```python
import functools

import jax
import jax.numpy as jnp
from jax import lax
from jax.experimental import pallas as pl
from jax.experimental.pallas import tpu as pltpu
from jax.sharding import PartitionSpec as P

PANEL = 256
BLOCK = 64
HIGH = lax.Precision.HIGHEST
F32 = jnp.float32


def combine(left_prod, right_prod):
    seg = left_prod.shape[1] // 4
    return (
        left_prod[:, seg : 2 * seg] * right_prod[:, 2 * seg : 3 * seg]
        + right_prod[:, seg : 2 * seg] * left_prod[:, 2 * seg : 3 * seg]
        + left_prod[:, 0:seg] * right_prod[:, 3 * seg : 4 * seg]
        + right_prod[:, 0:seg] * left_prod[:, 3 * seg : 4 * seg]
    )


def finish_kernel(grid_rows, grid_cols, block_ref, schur_ref, first_ref, out_ref, work, coef_ref, mixed):
    base = block_ref[:PANEL, :]
    work[:, :PANEL] = 0.5 * (base + base.T)
    rows = lax.broadcasted_iota(jnp.int32, (PANEL, PANEL), 0)
    cols = lax.broadcasted_iota(jnp.int32, (PANEL, PANEL), 1)
    work[:, PANEL:] = jnp.where(rows == cols, 1.0, 0.0).astype(F32)
    row = lax.broadcasted_iota(jnp.int32, (BLOCK, 1), 0)
    brow = lax.broadcasted_iota(jnp.int32, (BLOCK, BLOCK), 0)
    bcol = lax.broadcasted_iota(jnp.int32, (BLOCK, BLOCK), 1)
    eye = jnp.where(brow == bcol, 1.0, 0.0).astype(F32)
    for b in range(PANEL // BLOCK):
        lo = b * BLOCK
        hi = lo + BLOCK
        pair = jnp.concatenate([work[lo:hi, lo:hi], eye], axis=1)
        for k in range(BLOCK):
            pivot = pair[k : k + 1, :]
            scaled = pivot / pair[k : k + 1, k : k + 1]
            factor = jnp.where(row > k, pair[:, k : k + 1], 0.0)
            pair = pair - factor * scaled
        diag = jnp.sum(pair[:, :BLOCK] * eye, axis=1, keepdims=True)
        inv = pair[:, BLOCK:] / jnp.sqrt(diag)
        done = jnp.dot(inv, work[lo:hi, :], precision=HIGH, preferred_element_type=F32)
        work[lo:hi, :] = done
        if hi < PANEL:
            lower = done[:, :PANEL]
            step = lax.dot_general(
                lower, done, (((0,), (0,)), ((), ())), precision=HIGH, preferred_element_type=F32
            )
            work[hi:, :] = work[hi:, :] - step[hi:, :]
    inverse = work[:, PANEL:]
    coef_ref[:PANEL, :] = inverse
    ahead = lax.dot_general(
        block_ref[PANEL:, :],
        inverse,
        (((1,), (1,)), ((), ())),
        precision=HIGH,
        preferred_element_type=F32,
    )
    coef_ref[PANEL:, :] = jnp.dot(ahead, inverse, precision=HIGH, preferred_element_type=F32)
    slots = schur_ref.shape[0]
    height = PANEL // (grid_rows * grid_cols)
    groups = slots // (grid_rows * height)
    narrow = PANEL // grid_cols
    first = first_ref[...]
    ident = lax.broadcasted_iota(jnp.int32, (slots, PANEL), 0)
    both = lax.dot_general(
        schur_ref[:, :PANEL],
        coef_ref[...],
        (((1,), (1,)), ((), ())),
        precision=HIGH,
        preferred_element_type=F32,
    )
    mixed[:, :PANEL] = jnp.where(ident >= first, both[:, :PANEL], 0.0)
    mixed[:, PANEL:] = jnp.where(
        ident >= first + height, schur_ref[:, PANEL:] - both[:, PANEL:], 0.0
    )
    if height % 8:
        out_ref[...] = mixed[...]
        return
    run = 128 // narrow
    for prow in range(grid_rows):
        for half in range(2):
            for group in range(0, groups, run):
                tops = [((group + i) * grid_rows + prow) * height for i in range(run)]
                for pcol in range(grid_cols):
                    lo = half * PANEL + pcol * narrow
                    to = (half * groups + group) * narrow
                    out_ref[prow * grid_cols + pcol, :, to : to + 128] = jnp.concatenate(
                        [mixed[top : top + height, lo : lo + narrow] for top in tops], axis=1
                    )


def finish(panel_block, schur, first_slot, grid_rows, grid_cols):
    devices = grid_rows * grid_cols
    slots = schur.shape[0]
    height = PANEL // devices
    groups = slots // (grid_rows * height)
    narrow = PANEL // grid_cols
    tiled = height % 8 == 0
    shape = (devices, height, 2 * groups * narrow) if tiled else (slots, 2 * PANEL)
    out = pl.pallas_call(
        functools.partial(finish_kernel, grid_rows, grid_cols),
        out_shape=jax.ShapeDtypeStruct(shape, F32),
        in_specs=[pl.BlockSpec(memory_space=pltpu.VMEM)] * 3,
        out_specs=pl.BlockSpec(memory_space=pltpu.VMEM),
        scratch_shapes=[
            pltpu.VMEM((PANEL, 2 * PANEL), F32),
            pltpu.VMEM((2 * PANEL, PANEL), F32),
            pltpu.VMEM((slots, 2 * PANEL), F32),
        ],
        compiler_params=pltpu.CompilerParams(vmem_limit_bytes=24 * 1024 * 1024),
    )(panel_block, schur, jnp.full((1, PANEL), first_slot, jnp.int32))
    if tiled:
        return out
    out = out.reshape(groups, grid_rows, height, 2, grid_cols, narrow)
    return out.transpose(1, 4, 2, 3, 0, 5).reshape(devices, height, 2 * groups * narrow)


def gather_kernel(grid_rows, grid_cols, x_ref, out_ref, local_sem, send_sem, recv_sem):
    prow = lax.axis_index("prow")
    pcol = lax.axis_index("pcol")
    chip = pcol // 2
    core = pcol % 2
    across = grid_cols // 4
    side = chip // across
    place = chip % across

    def column(side_at, place_at, core_at):
        return (side_at * across + place_at) * 2 + core_at

    near = sorted(range(1, grid_rows), key=lambda s: (min(s, grid_rows - s), s))
    along = [(lax.rem(prow + s, grid_rows), pcol) for s in near]
    facing = (prow, column(1 - side, place, core))
    beside = [
        (prow, column(side, lax.rem(place + t, across), core)) for t in range(1, across)
    ]
    sibling = (prow, column(side, place, 1 - core))
    barrier = pltpu.get_barrier_semaphore()
    peers = along + [facing] + beside + [sibling]
    for peer in peers:
        pl.semaphore_signal(barrier, inc=1, device_id=peer, device_id_type=pl.DeviceIdType.MESH)
    pl.semaphore_wait(barrier, len(peers))

    sends = []

    def send(src, slot, peer):
        copy = pltpu.make_async_remote_copy(
            src_ref=src,
            dst_ref=out_ref.at[slot],
            send_sem=send_sem.at[len(sends)],
            recv_sem=recv_sem.at[slot],
            device_id=peer,
            device_id_type=pl.DeviceIdType.MESH,
        )
        copy.start()
        sends.append(copy)

    def arrive(slot):
        pltpu.make_async_remote_copy(
            src_ref=out_ref.at[slot],
            dst_ref=out_ref.at[slot],
            send_sem=send_sem.at[0],
            recv_sem=recv_sem.at[slot],
            device_id=sibling,
            device_id_type=pl.DeviceIdType.MESH,
        ).wait_recv()

    def slot_of(row, col, half):
        return (row * grid_cols + col) * 2 + half

    def pass_on(slot, to):
        arrive(slot)
        for peer in to:
            send(out_ref.at[slot], slot, peer)

    mine = slot_of(prow, pcol, 0)
    local = pltpu.make_async_copy(x_ref, out_ref.at[pl.ds(mine, 2)], local_sem)
    local.start()
    for half in range(2):
        for peer in [facing] + beside + along + [sibling]:
            send(x_ref.at[half], mine + half, peer)

    def from_plane(row):
        for half in range(2):
            slot = slot_of(row, facing[1], half)
            pass_on(slot, (beside if half == 0 else []) + [sibling])
            for peer in beside:
                slot = slot_of(row, peer[1], half)
                pass_on(slot, ([facing] if half == 1 else []) + [sibling])

    def from_corner(row):
        for t in range(1, across):
            col = column(1 - side, lax.rem(place + t, across), core)
            for half in range(2):
                pass_on(slot_of(row, col, half), [sibling])

    rows = [prow] + [peer[0] for peer in along]
    for step in range(grid_rows + 2):
        if 0 < step < grid_rows:
            for half in range(2):
                pass_on(slot_of(rows[step], pcol, half), [facing] + beside + [sibling])
        if 1 <= step <= grid_rows:
            from_plane(rows[step - 1])
        if 2 <= step:
            from_corner(rows[step - 2])
    for row in rows:
        for side_at in (side, 1 - side):
            for t in range(across):
                col = column(side_at, lax.rem(place + t, across), 1 - core)
                for half in range(2):
                    arrive(slot_of(row, col, half))
    local.wait()
    for copy in sends:
        copy.wait_send()


def gather(x, collective_id, tile):
    grid_rows = lax.axis_size("prow")
    grid_cols = lax.axis_size("pcol")
    devices = grid_rows * grid_cols
    rows, columns = x.shape
    if grid_cols % 4 or rows % (2 * tile):
        return lax.all_gather(x, ("prow", "pcol"), axis=0, tiled=True)
    across = grid_cols // 4
    count = 2 * (grid_rows - 1 + grid_rows * across + grid_rows * grid_cols // 2)
    count += 2 * grid_rows * (across - 1)
    out = pl.pallas_call(
        functools.partial(gather_kernel, grid_rows, grid_cols),
        out_shape=jax.ShapeDtypeStruct((2 * devices, rows // 2, columns), x.dtype),
        in_specs=[pl.BlockSpec(memory_space=pl.ANY)],
        out_specs=pl.BlockSpec(memory_space=pl.ANY),
        scratch_shapes=[
            pltpu.SemaphoreType.DMA,
            pltpu.SemaphoreType.DMA((count,)),
            pltpu.SemaphoreType.DMA((2 * devices,)),
        ],
        compiler_params=pltpu.CompilerParams(
            collective_id=collective_id, has_side_effects=True
        ),
    )(x.reshape(2, rows // 2, columns))
    return out.reshape(devices * rows, columns)


def body(left_vecs, right_vecs, primal, dual_inverse, owner_map, panel_index):
    devices = lax.axis_size(("prow", "pcol"))
    grid_rows = lax.axis_size("prow")
    grid_cols = lax.axis_size("pcol")
    height = PANEL // devices
    slots = left_vecs.shape[0]
    order = left_vecs.shape[1]
    feats = primal.shape[0]
    start = panel_index[0] * PANEL
    first_slot = start // devices
    wide = lax.broadcasted_iota(jnp.int32, (devices, height, height, devices), 0)
    perm = (wide == owner_map[None, None, None, :]) & (
        lax.broadcasted_iota(jnp.int32, wide.shape, 1)
        == lax.broadcasted_iota(jnp.int32, wide.shape, 2)
    )
    perm = perm.astype(jnp.bfloat16).reshape(PANEL, PANEL)
    perm32 = perm.astype(F32)

    panel_left = lax.dynamic_slice_in_dim(left_vecs, first_slot, 2 * height, 0)
    panel_right = lax.dynamic_slice_in_dim(right_vecs, first_slot, 2 * height, 0)
    own_vecs = jnp.concatenate([panel_left, panel_right], axis=0)
    panel_vecs = gather(own_vecs, 0, 16)
    matrices = jnp.concatenate([primal, dual_inverse], axis=0)
    raw = lax.dot_general(
        panel_vecs, matrices, (((1,), (1,)), ((), ())), preferred_element_type=F32
    )
    raw = raw.reshape(devices, 4, height, 2 * feats).transpose(1, 0, 2, 3)
    raw = raw.reshape(4, PANEL, 2, feats).astype(jnp.bfloat16)
    images = jnp.einsum("vkgf,kj->fgvj", raw, perm, preferred_element_type=F32)
    images = images.astype(jnp.bfloat16).reshape(feats, 8 * PANEL)
    piece = gather(images, 1, 16)
    left_prod = jnp.dot(left_vecs, piece, preferred_element_type=F32)
    right_prod = jnp.dot(right_vecs, piece, preferred_element_type=F32)
    schur = combine(left_prod, right_prod)

    own_panel = lax.dynamic_slice_in_dim(schur[:, :PANEL], first_slot, 2 * height, 0)
    panel_rows = gather(own_panel, 2, 8)
    panel_rows = panel_rows.reshape(devices, 2, height, PANEL).transpose(1, 0, 2, 3)
    panel_block = jnp.einsum(
        "kj,pkc->pjc",
        perm32,
        panel_rows.reshape(2, PANEL, PANEL),
        precision=HIGH,
        preferred_element_type=F32,
    ).reshape(2 * PANEL, PANEL)
    groups = slots // (grid_rows * height)
    narrow = PANEL // grid_cols
    outgoing = finish(panel_block, schur, first_slot, grid_rows, grid_cols)
    arrived = lax.all_to_all(outgoing, ("prow", "pcol"), split_axis=0, concat_axis=0, tiled=True)
    final = lax.dot_general(
        arrived.reshape(PANEL, groups * 2 * narrow),
        perm32,
        (((0,), (0,)), ((), ())),
        precision=HIGH,
        preferred_element_type=F32,
    )
    final = final.reshape(2, groups, narrow, PANEL).transpose(0, 2, 1, 3)
    final = final.reshape(2, narrow, groups * PANEL)
    return (final[0], final[1])


def solution(mesh):
    return jax.shard_map(
        body,
        mesh=mesh,
        in_specs=(
            P(("prow", "pcol"), None),
            P(("prow", "pcol"), None),
            P(("prow", "pcol"), None),
            P(("prow", "pcol"), None),
            P(),
            P(),
        ),
        out_specs=(P("pcol", "prow"), P("pcol", "prow")),
        check_vma=False,
    )
```
